32 devices in a mesh: dp: 8 (over z, y), ctx: 4 (over x, core).
Axes of the slice: x: 2, y: 2, z: 4, core: 2. Of those that a mesh axis runs over, the one named last changes fastest.
Arguments:
- hidden_in: bfloat16 [8, 512, 5376], P('dp', 'ctx'), may hold values from -30 to 30
- w_qkv: bfloat16 [5376, 512], P('ctx'), may hold values from -1 to 1
- d_attn: bfloat16 [8, 512, 256], P('dp', 'ctx'), may hold values from -6 to 6
- range_len: int32 [8, 4], P('dp', 'ctx'), may hold values from 96 to 128, as said below
- doc_ids: int32 [8, 512], P('dp', 'ctx'), may hold values from 0 to 1, never falling along the last dimension, each value on 1 to 384 neighbouring positions
Outputs:
- d_x: bfloat16 [8, 512, 5376], P('dp', 'ctx')
- d_w: float32 [5376, 512], P('ctx')
The draws below stay inside these ranges and needn't reach their ends.
Inputs may be any that keep to these rules, and one draw needn't show every extreme that they name: `range_len`: every range holds between 96 and 128 live tokens; in every sequence one range holds exactly 128 and another exactly 96.
All inputs are finite; a program needn't handle non-finite values.
Results may differ from the reference program's by a relative error of at most 0.015.
Values may be sent and summed in bfloat16 or wider, within the bound.
No kernel may reach another device: no remote copies, remote signals or barrier semaphores. Data moves between devices by JAX's collectives and lax.ppermute only.
A program may use at most 64 MiB of HBM per device.

```python
import math
import jax
import jax.numpy as jnp
import numpy as np
from jax import lax

D = 5376
HD = 128
WINDOW = 1024
QHEADS = 2
CAP = 128
SEQS = 8
BLOCKS = 4
SLOTS = 512
QKV = 512
MIN_LEN = 96


def draw_hidden_in(key, part):
    values = jnp.clip(jax.random.normal(key, (SEQS, SLOTS, D), jnp.float32), -6.0, 6.0)
    return values.astype(jnp.bfloat16)


def draw_w_qkv(key, part):
    scale = D ** (-0.5)
    whole = jax.random.normal(jax.random.fold_in(key, 5), (D, QKV), jnp.float32) * scale
    return jnp.clip(whole, -1.0, 1.0).astype(jnp.bfloat16)


def draw_range_len(key, part):
    lengths = jax.random.randint(key, (SEQS, BLOCKS), MIN_LEN, CAP + 1)
    chosen = jax.random.randint(jax.random.fold_in(key, 3), (SEQS, 1), 0, BLOCKS)
    other = (chosen + 1) % BLOCKS
    index = jnp.arange(BLOCKS, dtype=jnp.int32)[None, :]
    lengths = jnp.where(index == chosen, CAP, lengths)
    lengths = jnp.where(index == other, MIN_LEN, lengths)
    return lengths.astype(jnp.int32)


def steps_of(key, dims, cuts, low, largest):
    def one(dim, blocks):
        heights = jax.random.uniform(jax.random.fold_in(jax.random.fold_in(key, 6), dim), (blocks,), jnp.float32, low / len(cuts), largest / len(cuts))
        return jnp.repeat(jnp.exp(heights), dims[dim] // blocks).reshape((-1,) + (1,) * (len(dims) - dim - 1))

    loudness = one(*cuts[0])
    for cut in cuts[1:]:
        loudness = loudness * one(*cut)
    return loudness


def length_profile(amount, total, reach, slope):
    portions = [(1 << 20) // math.isqrt(standing ** slope) + 1 for standing in range(2, amount + 1)]
    surplus, holding = total - reach - (amount - 1), [1] * (amount - 1)
    while surplus > 0:
        candidates = [i for i in range(amount - 1) if holding[i] < reach]
        pool, remaining = sum([portions[i] for i in candidates]), surplus
        for i in candidates:
            addition = min(reach - holding[i], max(1, remaining * portions[i] // pool), surplus)
            holding[i] = holding[i] + addition
            surplus = surplus - addition
    return np.array([reach] + holding)


def ragged(stream_key, amount, total, reach, slope):
    if amount == 2:
        one = jax.random.randint(stream_key, (), max(1, total - reach), min(reach, total - 1) + 1)
        return jnp.stack([one, total - one])
    sizes = jnp.asarray(length_profile(amount, total, reach, slope), jnp.int32)
    twos = (amount - 1) // 2
    donor, receiver = sizes[1:1 + 2 * twos:2], sizes[2:2 + 2 * twos:2]
    slack = jnp.minimum(donor - 1, reach - receiver)
    shifted = jax.random.randint(jax.random.fold_in(stream_key, 1), (twos,), 0, 1 << 20) % (slack + 1)
    sizes = sizes.at[1:1 + 2 * twos:2].set(donor - shifted).at[2:2 + 2 * twos:2].set(receiver + shifted)
    return sizes[jax.random.permutation(jax.random.fold_in(stream_key, 2), amount)]


def centred(stream_key, extent, deviation, reach, shards=(), kind=jnp.bfloat16):
    result = deviation * jax.random.normal(stream_key, extent, jnp.float32)
    if shards:
        result = result * steps_of(stream_key, extent, shards, -0.22, 0.18)
    return jnp.clip(result, -reach, reach).astype(kind)


def setup_inputs(seed: int = 0) -> dict:
    splits = jax.random.split(jax.random.key(seed), 6)
    return {
        "hidden_in": draw_hidden_in(jax.random.fold_in(splits[5], 71), 0),
        "w_qkv": draw_w_qkv(jax.random.fold_in(splits[5], 71), 0),
        "d_attn": centred(splits[2], (SEQS, SLOTS, QHEADS * HD), 1.0, 6.0, ((0, 8), (1, 4))),
        "range_len": draw_range_len(jax.random.fold_in(splits[5], 71), 0),
        "doc_ids": jax.vmap(lambda own: jnp.searchsorted(jnp.cumsum(ragged(own, 2, SLOTS, 3 * SLOTS // 4, 0)), jnp.arange(SLOTS), side="right"))(jax.random.split(splits[4], SEQS)).reshape((SEQS, SLOTS)).astype(jnp.int32),
    }


score_scale = 168.0 ** -0.5
neg_fill = -1.0e30


def rotary_tables(positions, head_size):
    half = head_size // 2
    freqs = 10000.0 ** (-(jnp.arange(half, dtype=jnp.float32) * 2.0) / head_size)
    angles = positions.astype(jnp.float32)[:, None] * freqs[None, :]
    return jnp.cos(angles), jnp.sin(angles)


def rotate(values, cosine, sine, sign):
    half = values.shape[-1] // 2
    first = values[..., :half]
    second = values[..., half:]
    return jnp.concatenate([first * cosine - sign * second * sine, second * cosine + sign * first * sine], axis=-1)


def allowed_pairs(query_meta, key_meta):
    qpos = query_meta[:, 0][:, None]
    kpos = key_meta[:, 0][None, :]
    same_doc = query_meta[:, 1][:, None] == key_meta[:, 1][None, :]
    both_live = (query_meta[:, 2][:, None] == 1) & (key_meta[:, 2][None, :] == 1)
    return both_live & same_doc & (kpos <= qpos) & (qpos - kpos < WINDOW)


def one_sequence(tokens, w_qkv, grads, lengths, docs):
    slot = jnp.arange(SLOTS, dtype=jnp.int32)
    block = slot // CAP
    offset = slot - block * CAP
    starts = (jnp.cumsum(lengths) - lengths).astype(jnp.int32)
    positions = starts[block] + offset
    live = offset < lengths[block]
    meta = jnp.stack([positions, docs.astype(jnp.int32), live.astype(jnp.int32)], axis=1)
    cosine, sine = rotary_tables(positions, HD)
    nq = QHEADS * HD
    proj = jnp.dot(tokens, w_qkv, preferred_element_type=jnp.float32)
    queries = rotate(proj[:, :nq].reshape(SLOTS, QHEADS, HD), cosine[:, None, :], sine[:, None, :], 1.0).astype(jnp.bfloat16)
    keys = rotate(proj[:, nq:nq + HD], cosine, sine, 1.0).astype(jnp.bfloat16)
    values = proj[:, nq + HD:].astype(jnp.bfloat16)
    grad_out = grads.reshape(SLOTS, QHEADS, HD)
    qf = queries.astype(jnp.float32)
    kf = keys.astype(jnp.float32)
    vf = values.astype(jnp.float32)
    gf = grad_out.astype(jnp.float32)
    allowed = allowed_pairs(meta, meta)[None]
    scores = score_scale * jnp.einsum("qhd,kd->hqk", qf, kf)
    dots = jnp.einsum("qhd,kd->hqk", gf, vf)
    top = jnp.max(jnp.where(allowed, scores, neg_fill), axis=2)
    expo = jnp.where(allowed, jnp.exp(scores - top[:, :, None]), 0.0)
    total = jnp.sum(expo, axis=2)
    weighted = jnp.sum(expo * dots, axis=2)
    live_rows = live[None, :]
    safe_total = jnp.where(live_rows, total, 1.0)
    lse = jnp.where(live_rows, top + jnp.log(safe_total), 0.0)
    delta = jnp.where(live_rows, weighted / safe_total, 0.0)
    probs = jnp.where(allowed, jnp.exp(scores - lse[:, :, None]), 0.0)
    mixed = (probs * (dots - delta[:, :, None])).astype(jnp.bfloat16).astype(jnp.float32)
    probs16 = probs.astype(jnp.bfloat16).astype(jnp.float32)
    dq = score_scale * jnp.einsum("hqk,kd->qhd", mixed, kf)
    dk = score_scale * jnp.einsum("hqk,qhd->kd", mixed, qf)
    dv = jnp.einsum("hqk,qhd->kd", probs16, gf)
    dq_pre = rotate(dq, cosine[:, None, :], sine[:, None, :], -1.0).reshape(SLOTS, nq)
    dk_pre = rotate(dk, cosine, sine, -1.0)
    d_proj = jnp.concatenate([dq_pre, dk_pre, dv], axis=1).astype(jnp.bfloat16)
    d_x = jnp.dot(d_proj, w_qkv.T, preferred_element_type=jnp.float32).astype(jnp.bfloat16)
    d_w = jnp.dot(tokens.T, d_proj, preferred_element_type=jnp.float32)
    return d_x, d_w


def reference(hidden_in, w_qkv, d_attn, range_len, doc_ids):
    def step(carry, item):
        tokens, grads, lengths, docs = item
        d_x, d_w = one_sequence(tokens, w_qkv, grads, lengths, docs)
        return carry + d_w, d_x

    start = jnp.zeros((D, QKV), jnp.float32)
    d_w, d_x = lax.scan(step, start, (hidden_in, d_attn, range_len, doc_ids))
    return d_x, d_w
```

```python
import functools

import jax
import jax.numpy as jnp
from jax import lax
from jax.experimental import pallas as pl
from jax.experimental.pallas import tpu as pltpu
from jax.sharding import PartitionSpec as P

HD = 128
WINDOW = 1024
QHEADS = 2
NQ = QHEADS * HD
LANES = 128
QUAD = 4
SPLITS = 2
EXTRA = 16
SUM_COST = 8_000_000_000
DOC_STEP = 1 << 20
VMEM_BYTES = 48 * 1024 * 1024

score_scale = 168.0 ** (-0.5)
neg_fill = -1e30
f32 = jnp.float32
bf16 = jnp.bfloat16


def swap(value, axis, mask):
    count = lax.axis_size(axis)
    return lax.ppermute(value, axis, [(i, i ^ mask) for i in range(count)])


def after(value, *others):
    return lax.optimization_barrier((value, others))[0]


def rotate(values, cosine, sine):
    return values * cosine + pltpu.roll(values, HD // 2, 1) * sine


def call(kernel, out_shape, scratch=(), flops=0, moved=0, **more):
    return pl.pallas_call(
        kernel,
        out_shape=out_shape,
        scratch_shapes=list(scratch),
        compiler_params=pltpu.CompilerParams(vmem_limit_bytes=VMEM_BYTES),
        cost_estimate=pl.CostEstimate(flops=flops, bytes_accessed=moved, transcendentals=0),
        **more,
    )


def shape(dims, dtype):
    return jax.ShapeDtypeStruct(dims, dtype)


class Sizes:
    def __init__(self, tokens, w_qkv):
        self.n = lax.axis_size("ctx")
        self.cap, self.width = tokens.shape
        self.rows, self.qkv = w_qkv.shape
        self.slots = self.n * self.cap
        tiles = self.width // LANES
        need = 1
        for c in range(self.n):
            low, high = (c * self.rows, (c + 1) * self.rows)
            need = max(need, -(-high // LANES) - low // LANES)
        self.win = need * LANES
        self.last = tiles - need
        self.chunk = -(-self.rows // (QUAD * 16)) * 16

    def first(self, c):
        return pl.multiple_of(jnp.minimum(c * self.rows // LANES, self.last) * LANES, LANES)

    def inset(self, c):
        return pl.multiple_of(c * self.rows - self.first(c), 16)

    def block(self, k):
        return pl.ds(pl.multiple_of((lax.axis_index("ctx") ^ k) * self.cap, self.cap), self.cap)

    def own_window(self, x_ref):
        return x_ref[:, pl.ds(self.first(lax.axis_index("ctx")), self.win)]


def windows_kernel(z, x_ref, *refs):
    outs, sems = (refs[: z.n - 1], refs[z.n - 1])
    me = lax.axis_index("ctx")
    copies = [
        pltpu.make_async_copy(x_ref.at[:, pl.ds(z.first(me ^ k), z.win)], outs[k - 1], sems.at[k - 1])
        for k in range(1, z.n)
    ]
    for copy in copies:
        copy.start()
    for copy in copies:
        copy.wait()


def pad_kernel(z, w_ref, pad):
    pad[...] = jnp.zeros_like(pad)
    pad[pl.ds(z.inset(lax.axis_index("ctx")), z.rows), :] = w_ref[...]


def spread_kernel(z, order, packs, grads, qrow, kcol, poscol):
    me = lax.axis_index("ctx")
    rows = lax.broadcasted_iota(jnp.int32, (z.n, z.cap), 0)
    docs = jnp.zeros((z.n, z.cap), f32)
    lens = jnp.zeros((z.n, z.cap), f32)
    tall = z.cap + EXTRA
    for place, k in enumerate(order):
        at = place * tall
        grads[z.block(k), :] = packs[at : at + z.cap, :]
        extra = packs[at + z.cap : at + tall, :].astype(f32)[:1]
        docs = jnp.where(rows == (me ^ k), extra[:, : z.cap], docs)
        lens = jnp.where(rows == (me ^ k), extra[:, z.cap : 2 * z.cap], lens)
    docs = docs.astype(jnp.int32)
    lens = lens.astype(jnp.int32)
    offset = lax.broadcasted_iota(jnp.int32, (z.n, z.cap), 1)
    start = jnp.zeros((1, z.cap), jnp.int32)
    for c in range(z.n):
        pos = start + offset[c : c + 1]
        live = offset[c : c + 1] < lens[c : c + 1]
        mark = docs[c : c + 1] * DOC_STEP + pos
        qrow[c : c + 1, :] = jnp.where(live, mark, -DOC_STEP)
        at = slice(c * z.cap, (c + 1) * z.cap)
        key = jnp.where(live, mark, 4 * DOC_STEP).astype(f32)
        kcol[at, :] = jnp.broadcast_to(key, (LANES, z.cap)).T.astype(jnp.int32)
        poscol[at, :] = jnp.broadcast_to(pos.astype(f32), (LANES, z.cap)).T
        start = start + lens[c : c + 1]


def near_kernel(z, x_ref, x1_ref, w_ref, keep, send):
    keep[...] = jnp.dot(z.own_window(x_ref), w_ref[...], preferred_element_type=f32)
    send[...] = jnp.dot(x1_ref[...], w_ref[...], preferred_element_type=f32).astype(bf16)


def far_kernel(z, *refs):
    xs, (w_ref, _, keep, send) = (refs[: z.n - 2], refs[z.n - 2 :])
    for k in range(0, z.n - 2, 2):
        at = slice(k // 2 * z.cap, (k // 2 + 1) * z.cap)
        send[at, :] = jnp.dot(xs[k + 1][...], w_ref[...], preferred_element_type=f32).astype(bf16)
        keep[at, :] = jnp.dot(xs[k][...], w_ref[...], preferred_element_type=f32)


def transpose_kernel(z, x_ref, *refs):
    xs, out = (refs[: z.n - 1], refs[z.n - 1])
    out[:, z.block(0)] = z.own_window(x_ref).T
    for k in range(1, z.n):
        out[:, z.block(k)] = xs[k - 1][...].T


def rotary_kernel(z, *refs):
    count = z.n // 2
    kept, came, (cos_ref, sin_ref, out) = (refs[:count], refs[count : 2 * count], refs[2 * count :])
    for i in range(count):
        proj = kept[i][...].astype(f32) + came[i][...].astype(f32)
        rows = z.block(2 * i)
        at = slice(i * z.cap, (i + 1) * z.cap)
        cosine, sine = (cos_ref[rows, :], sin_ref[rows, :])
        for h in range(QHEADS + 1):
            cols = slice(h * HD, (h + 1) * HD)
            out[at, cols] = rotate(proj[:, cols], cosine, sine).astype(bf16)
        out[at, NQ + HD :] = proj[:, NQ + HD :].astype(bf16)


def attention_kernel(z, own, other, g_ref, qrow, kcol, cos_ref, sin_ref, out, qkv, dk, dv):
    block = z.cap
    for k in range(z.n):
        source = other if k & 1 else own
        qkv[z.block(k), :] = source[k // 2 * block : (k // 2 + 1) * block, :]
    kt = qkv[:, NQ : NQ + HD].astype(f32).T.astype(bf16)
    for i in range(z.n):
        rows = slice(i * block, (i + 1) * block)
        extent = (i + 1) * block
        q2 = jnp.concatenate([qkv[rows, h * HD : (h + 1) * HD] for h in range(QHEADS)], axis=0)
        g2 = jnp.concatenate([g_ref[rows, h * HD : (h + 1) * HD] for h in range(QHEADS)], axis=0)
        keys = qkv[:extent, NQ : NQ + HD]
        values = qkv[:extent, NQ + HD :]
        nt = (((1,), (1,)), ((), ()))
        scores = lax.dot_general(keys, q2, nt, preferred_element_type=f32)
        dots = lax.dot_general(values, g2, nt, preferred_element_type=f32)
        query = qrow[i : i + 1, :]
        behind = query - kcol[:extent, :]
        allowed = (behind >= 0) & (behind < WINDOW)
        allowed = jnp.concatenate([allowed] * QHEADS, axis=1)
        query = jnp.concatenate([query] * QHEADS, axis=1)
        scores = jnp.where(allowed, scores, neg_fill)
        top = jnp.max(scores, axis=0, keepdims=True)
        expo = jnp.exp((scores - top) * score_scale)
        total = jnp.sum(expo, axis=0, keepdims=True)
        weighted = jnp.sum(expo * dots, axis=0, keepdims=True)
        inverse = jnp.where(query >= 0, 1.0 / total, 0.0)
        delta = weighted * inverse
        probs = expo * inverse
        mixed = (probs * (dots - delta)).astype(bf16)
        probs = probs.astype(bf16)
        dkey = jnp.dot(mixed, q2, preferred_element_type=f32)
        dval = jnp.dot(probs, g2, preferred_element_type=f32)
        before = i * block
        if before:
            dk[:before, :] += dkey[:before]
            dv[:before, :] += dval[:before]
        dk[before:extent, :] = dkey[before:]
        dv[before:extent, :] = dval[before:]
        dq = score_scale * jnp.dot(kt[:, :extent], mixed, preferred_element_type=f32)
        for h in range(QHEADS):
            dq_h = dq[:, h * block : (h + 1) * block].T
            out[rows, h * HD : (h + 1) * HD] = rotate(dq_h, cos_ref[rows, :], -sin_ref[rows, :]).astype(bf16)
    out[:, NQ : NQ + HD] = rotate(score_scale * dk[...], cos_ref[...], -sin_ref[...]).astype(bf16)
    out[:, NQ + HD :] = dv[...].astype(bf16)


def weight_kernel(z, xt, g_ref, *refs):
    pieces, whole = (refs[:-1], refs[-1])
    if whole.shape[0] > z.win:
        whole[z.win :, :] = jnp.zeros_like(whole[z.win :, :])
    inset = z.inset(lax.axis_index("ctx"))
    mine = lax.axis_index("dp") & (QUAD - 1)
    wide = z.qkv // SPLITS
    for s in range(SPLITS):
        cols = slice(s * wide, (s + 1) * wide)
        whole[: z.win, :] = jnp.dot(xt[...], g_ref[:, cols], preferred_element_type=f32)
        for k in range(QUAD):
            at = pl.multiple_of(inset + (mine ^ k) * z.chunk, 16)
            pieces[s * QUAD + k][...] = whole[pl.ds(at, z.chunk), :].astype(bf16)


def sum_kernel(*refs):
    refs[-1][...] = functools.reduce(lambda a, b: a + b, [r[...].astype(f32) for r in refs[:-1]]).astype(bf16)


def total_of(*pieces):
    return call(sum_kernel, shape(pieces[0].shape, bf16), flops=SUM_COST)(*pieces)


def inputs_kernel(z, g_ref, w_ref, near, far):
    for k in range(z.n):
        target = near if k < z.n // 2 else far
        at = k % (z.n // 2) * z.cap
        target[at : at + z.cap, :] = lax.dot_general(
            g_ref[z.block(k), :], w_ref[...], (((1,), (1,)), ((), ())), preferred_element_type=f32
        ).astype(bf16)


def place_weight_kernel(z, exact, first, *refs):
    pieces, out, whole = (refs[:QUAD], refs[-2], refs[-1])
    mine = lax.axis_index("dp") & (QUAD - 1)
    target = out if exact else whole
    for k in range(QUAD):
        at = pl.multiple_of((mine ^ k) * z.chunk, 16)
        target[pl.ds(at, z.chunk), :] = pieces[k][...].astype(f32)
    if not exact:
        out[...] = whole[: z.rows, :]


def place_weights(z, split, pieces, before):
    wide = z.qkv // SPLITS
    exact = QUAD * z.chunk == z.rows
    whole = lambda: pl.BlockSpec(memory_space=pltpu.VMEM)
    specs = [whole() for _ in pieces]
    more = {}
    if before is not None:
        specs.append(pl.BlockSpec(memory_space=pl.ANY))
        more["input_output_aliases"] = {QUAD: 0}
        pieces = [*pieces, before]
    return call(
        functools.partial(place_weight_kernel, z, exact, before is None),
        shape((z.rows, z.qkv), f32),
        [pltpu.VMEM((16, LANES) if exact else (QUAD * z.chunk, wide), f32)],
        flops=SUM_COST,
        grid=(1,),
        in_specs=specs,
        out_specs=pl.BlockSpec((z.rows, wide), lambda i: (0, split)),
        **more,
    )(*pieces)


def place_inputs_kernel(z, items, *refs):
    arrays, out = (refs[:-1], refs[-1])
    me = lax.axis_index("ctx")
    out[...] = jnp.zeros_like(out)
    for which, at, source in items:
        cols = pl.ds(z.first(me ^ source), z.win)
        out[:, cols] = out[:, cols] + arrays[which][at : at + z.cap, :]


def gather_packs(pack, n, first):
    order, mask = ([0], n // 2)
    came = first
    while mask:
        pack = jnp.concatenate([pack, came], axis=0)
        order = order + [k ^ mask for k in order]
        mask //= 2
        if mask:
            came = swap(pack, "ctx", mask)
    return pack, order


def exchange_inputs(z, near, far):
    arrays = [near]
    held = {(k, 0): (0, k * z.cap) for k in range(z.n // 2)}
    mask, sent = (z.n // 2, [(k, 0) for k in range(z.n // 2, z.n)])
    parcel = far
    while True:
        arrays.append(swap(parcel, "ctx", mask))
        for i, (k, j) in enumerate(sent):
            held[k ^ mask, j ^ mask] = (len(arrays) - 1, i * z.cap)
        mask //= 2
        if not mask:
            break
        sent = sorted(item for item in held if item[0] & mask)
        spots = [held.pop(item) for item in sent]
        parcel = jnp.concatenate([arrays[which][at : at + z.cap] for which, at in spots], axis=0)
    return arrays, [(which, at, j) for (k, j), (which, at) in sorted(held.items())]


def body(hidden_in, w_qkv, d_attn, range_len, doc_ids):
    tokens = hidden_in[0]
    z = Sizes(tokens, w_qkv)
    n, cap, slots, qkv, win = (z.n, z.cap, z.slots, z.qkv, z.win)
    any_spec = pl.BlockSpec(memory_space=pl.ANY)
    vmem_spec = pl.BlockSpec(memory_space=pltpu.VMEM)
    hbm_spec = pl.BlockSpec(memory_space=pltpu.HBM)

    extra = jnp.concatenate([doc_ids[0], jnp.broadcast_to(range_len[0, 0], (cap,))]).astype(bf16)
    pack = jnp.concatenate([d_attn[0], jnp.broadcast_to(extra[None], (EXTRA, NQ))], axis=0)
    cut = call(
        functools.partial(windows_kernel, z),
        [shape((cap, win), bf16)] * (n - 1),
        [pltpu.SemaphoreType.DMA((n - 1,))],
        moved=6 * cap * win,
        in_specs=[hbm_spec],
        out_specs=[any_spec] * (n - 1),
    )(tokens)
    xs = [swap(cut[k - 1], "ctx", k) for k in range(1, n)]
    pack_came = swap(pack, "ctx", n // 2)
    w_pad = call(functools.partial(pad_kernel, z), shape((win, qkv), bf16), moved=4 * win * qkv)(w_qkv)
    keep0, send0 = call(
        functools.partial(near_kernel, z),
        [shape((cap, qkv), f32), shape((cap, qkv), bf16)],
        flops=4 * cap * win * qkv,
        moved=4 * win * (cap + qkv),
    )(tokens, xs[0], w_pad)
    sum0 = keep0 + swap(send0, "ctx", 1).astype(f32)
    far_rows = (n // 2 - 1) * cap
    half0 = sum0.astype(bf16)
    cross0 = swap(half0, "ctx", 2)
    packs, order = gather_packs(pack, n, after(pack_came, sum0))
    grads, qrow, kcol, poscol = call(
        functools.partial(spread_kernel, z, order),
        [
            shape((slots, NQ), bf16),
            shape((n, cap), jnp.int32),
            shape((slots, LANES), jnp.int32),
            shape((slots, HD), f32),
        ],
        moved=8 * slots * NQ,
    )(packs)
    lane = jnp.arange(HD, dtype=jnp.int32)
    freqs = 10000.0 ** (-((lane % (HD // 2)).astype(f32) * 2.0) / HD)
    angles = poscol * freqs[None, :]
    cosine = jnp.cos(angles)
    sine = jnp.where(lane < HD // 2, -1.0, 1.0)[None, :] * jnp.sin(angles)

    keep1, send1 = call(
        functools.partial(far_kernel, z),
        [shape((far_rows, qkv), f32), shape((far_rows, qkv), bf16)],
        flops=4 * far_rows * win * qkv,
        moved=4 * win * (2 * far_rows + qkv),
        in_specs=[vmem_spec] * (n - 1) + [any_spec],
    )(*xs[1:], w_pad, half0)
    sum1 = keep1 + swap(send1, "ctx", 1).astype(f32)
    cross1 = swap(sum1.astype(bf16), "ctx", 2)
    kept = [sum0] + [sum1[i * cap : (i + 1) * cap] for i in range(n // 2 - 1)]
    came = [cross0] + [cross1[i * cap : (i + 1) * cap] for i in range(n // 2 - 1)]
    came = [came[i ^ 1] for i in range(n // 2)]
    mask = 4
    while mask < n:
        both = jnp.concatenate([a + b.astype(f32) for a, b in zip(kept, came)], axis=0)
        crossed = swap(both.astype(bf16), "ctx", mask)
        kept = [both[i * cap : (i + 1) * cap] for i in range(n // 2)]
        came = [crossed[i * cap : (i + 1) * cap] for i in range(n // 2)]
        came = [came[i ^ (mask // 2)] for i in range(n // 2)]
        mask *= 2
    xt = call(functools.partial(transpose_kernel, z), shape((win, slots), bf16), moved=4 * win * slots)(tokens, *xs)
    mine = call(functools.partial(rotary_kernel, z), shape((slots // 2, qkv), bf16), moved=4 * slots * qkv)(
        *kept, *came, cosine, sine
    )
    theirs = swap(mine, "ctx", 1)
    d_proj = call(
        functools.partial(attention_kernel, z),
        shape((slots, qkv), bf16),
        [pltpu.VMEM((slots, qkv), bf16), pltpu.VMEM((slots, HD), f32), pltpu.VMEM((slots, HD), f32)],
        flops=20 * slots * slots * HD,
        moved=8 * slots * qkv,
    )(mine, theirs, grads, qrow, kcol, cosine, sine)

    wide = qkv // SPLITS
    deep = max(win, win - z.rows + QUAD * z.chunk)
    parts = call(
        functools.partial(weight_kernel, z),
        [shape((z.chunk, wide), bf16)] * (QUAD * SPLITS),
        [pltpu.VMEM((deep, wide), f32)],
        flops=2 * win * slots * qkv,
        moved=4 * win * slots,
    )(xt, d_proj)
    sums = []
    for s in range(SPLITS):
        own = parts[s * QUAD : (s + 1) * QUAD]
        pieces = [own[0]] + [swap(own[k], "dp", k) for k in range(1, QUAD)]
        sums.append(total_of(*pieces))
    near, far = call(
        functools.partial(inputs_kernel, z),
        [shape((slots // 2, win), bf16)] * 2,
        flops=2 * win * slots * qkv,
        moved=4 * win * slots,
    )(d_proj, w_pad)
    totals = []
    for s in range(SPLITS):
        part, mask = (sums[s], QUAD)
        while mask < lax.axis_size("dp"):
            part = total_of(part, swap(part, "dp", mask))
            mask *= 2
        totals.append(part)
    arrays, items = exchange_inputs(z, near, far)
    d_w = None
    for s in range(SPLITS):
        d_w = place_weights(z, s, [totals[s]] + [swap(totals[s], "dp", k) for k in range(1, QUAD)], d_w)
    d_x = call(
        functools.partial(place_inputs_kernel, z, items), shape((cap, z.width), bf16), moved=4 * cap * z.width
    )(*arrays)
    return (d_x[None], d_w)


def solution(mesh):
    return jax.shard_map(
        body,
        mesh=mesh,
        in_specs=(
            P("dp", "ctx", None),
            P("ctx", None),
            P("dp", "ctx", None),
            P("dp", "ctx"),
            P("dp", "ctx"),
        ),
        out_specs=(P("dp", "ctx", None), P("ctx", None)),
        check_vma=False,
    )
```

```python
import functools

import jax
import jax.numpy as jnp
from jax import lax
from jax.experimental import pallas as pl
from jax.experimental.pallas import tpu as pltpu
from jax.sharding import PartitionSpec as P

HD = 128
WINDOW = 1024
QHEADS = 2
NQ = QHEADS * HD
LANES = 128
QUAD = 4
SPLITS = 2
EXTRA = 16
SUM_COST = 8_000_000_000
DOC_STEP = 1 << 20
VMEM_BYTES = 48 * 1024 * 1024

score_scale = 168.0 ** (-0.5)
neg_fill = -1e30
f32 = jnp.float32
bf16 = jnp.bfloat16


def swap(value, axis, mask):
    count = lax.axis_size(axis)
    return lax.ppermute(value, axis, [(i, i ^ mask) for i in range(count)])


def after(value, *others):
    return lax.optimization_barrier((value, others))[0]


def rotate(values, cosine, sine):
    return values * cosine + pltpu.roll(values, HD // 2, 1) * sine


def call(kernel, out_shape, scratch=(), flops=0, moved=0, **more):
    return pl.pallas_call(
        kernel,
        out_shape=out_shape,
        scratch_shapes=list(scratch),
        compiler_params=pltpu.CompilerParams(vmem_limit_bytes=VMEM_BYTES),
        cost_estimate=pl.CostEstimate(flops=flops, bytes_accessed=moved, transcendentals=0),
        **more,
    )


def shape(dims, dtype):
    return jax.ShapeDtypeStruct(dims, dtype)


class Sizes:
    def __init__(self, tokens, w_qkv):
        self.n = lax.axis_size("ctx")
        self.cap, self.width = tokens.shape
        self.rows, self.qkv = w_qkv.shape
        self.slots = self.n * self.cap
        tiles = self.width // LANES
        need = 1
        for c in range(self.n):
            low, high = (c * self.rows, (c + 1) * self.rows)
            need = max(need, -(-high // LANES) - low // LANES)
        self.win = need * LANES
        self.last = tiles - need
        self.chunk = -(-self.rows // (QUAD * 16)) * 16

    def first(self, c):
        return pl.multiple_of(jnp.minimum(c * self.rows // LANES, self.last) * LANES, LANES)

    def inset(self, c):
        return pl.multiple_of(c * self.rows - self.first(c), 16)

    def block(self, k):
        return pl.ds(pl.multiple_of((lax.axis_index("ctx") ^ k) * self.cap, self.cap), self.cap)

    def own_window(self, x_ref):
        return x_ref[:, pl.ds(self.first(lax.axis_index("ctx")), self.win)]


def windows_kernel(z, x_ref, *refs):
    outs, sems = (refs[: z.n - 1], refs[z.n - 1])
    me = lax.axis_index("ctx")
    copies = [
        pltpu.make_async_copy(x_ref.at[:, pl.ds(z.first(me ^ k), z.win)], outs[k - 1], sems.at[k - 1])
        for k in range(1, z.n)
    ]
    for copy in copies:
        copy.start()
    for copy in copies:
        copy.wait()


def pad_kernel(z, w_ref, pad):
    pad[...] = jnp.zeros_like(pad)
    pad[pl.ds(z.inset(lax.axis_index("ctx")), z.rows), :] = w_ref[...]


def spread_kernel(z, order, packs, grads, qrow, kcol, poscol):
    me = lax.axis_index("ctx")
    rows = lax.broadcasted_iota(jnp.int32, (z.n, z.cap), 0)
    docs = jnp.zeros((z.n, z.cap), f32)
    lens = jnp.zeros((z.n, z.cap), f32)
    tall = z.cap + EXTRA
    for place, k in enumerate(order):
        at = place * tall
        grads[z.block(k), :] = packs[at : at + z.cap, :]
        extra = packs[at + z.cap : at + tall, :].astype(f32)[:1]
        docs = jnp.where(rows == (me ^ k), extra[:, : z.cap], docs)
        lens = jnp.where(rows == (me ^ k), extra[:, z.cap : 2 * z.cap], lens)
    docs = docs.astype(jnp.int32)
    lens = lens.astype(jnp.int32)
    offset = lax.broadcasted_iota(jnp.int32, (z.n, z.cap), 1)
    start = jnp.zeros((1, z.cap), jnp.int32)
    for c in range(z.n):
        pos = start + offset[c : c + 1]
        live = offset[c : c + 1] < lens[c : c + 1]
        mark = docs[c : c + 1] * DOC_STEP + pos
        qrow[c : c + 1, :] = jnp.where(live, mark, -DOC_STEP)
        at = slice(c * z.cap, (c + 1) * z.cap)
        key = jnp.where(live, mark, 4 * DOC_STEP).astype(f32)
        kcol[at, :] = jnp.broadcast_to(key, (LANES, z.cap)).T.astype(jnp.int32)
        poscol[at, :] = jnp.broadcast_to(pos.astype(f32), (LANES, z.cap)).T
        start = start + lens[c : c + 1]


def near_kernel(z, x_ref, x1_ref, w_ref, keep, send):
    keep[...] = jnp.dot(z.own_window(x_ref), w_ref[...], preferred_element_type=f32)
    send[...] = jnp.dot(x1_ref[...], w_ref[...], preferred_element_type=f32).astype(bf16)


def odd_kernel(z, *refs):
    xs, (w_ref, _, send) = (refs[:-3], refs[-3:])
    for i, x_ref in enumerate(xs):
        at = slice(i * z.cap, (i + 1) * z.cap)
        send[at, :] = jnp.dot(x_ref[...], w_ref[...], preferred_element_type=f32).astype(bf16)


def even_kernel(z, *refs):
    xs, (w_ref, came, total, send) = (refs[:-4], refs[-4:])
    for i, x_ref in enumerate(xs):
        at = slice(i * z.cap, (i + 1) * z.cap)
        both = jnp.dot(x_ref[...], w_ref[...], preferred_element_type=f32) + came[at, :].astype(f32)
        total[at, :] = both
        send[at, :] = both.astype(bf16)


def transpose_kernel(z, x_ref, *refs):
    xs, out = (refs[: z.n - 1], refs[z.n - 1])
    out[:, z.block(0)] = z.own_window(x_ref).T
    for k in range(1, z.n):
        out[:, z.block(k)] = xs[k - 1][...].T


def rotary_kernel(z, *refs):
    count = z.n // 2
    kept, came, (cos_ref, sin_ref, out) = (refs[:count], refs[count : 2 * count], refs[2 * count :])
    for i in range(count):
        proj = kept[i][...].astype(f32) + came[i][...].astype(f32)
        rows = z.block(2 * i)
        at = slice(i * z.cap, (i + 1) * z.cap)
        cosine, sine = (cos_ref[rows, :], sin_ref[rows, :])
        for h in range(QHEADS + 1):
            cols = slice(h * HD, (h + 1) * HD)
            out[at, cols] = rotate(proj[:, cols], cosine, sine).astype(bf16)
        out[at, NQ + HD :] = proj[:, NQ + HD :].astype(bf16)


def attention_kernel(z, own, other, g_ref, qrow, kcol, cos_ref, sin_ref, out, qkv, dk, dv):
    block = z.cap
    for k in range(z.n):
        source = other if k & 1 else own
        qkv[z.block(k), :] = source[k // 2 * block : (k // 2 + 1) * block, :]
    kt = qkv[:, NQ : NQ + HD].astype(f32).T.astype(bf16)
    for i in range(z.n):
        rows = slice(i * block, (i + 1) * block)
        extent = (i + 1) * block
        q2 = jnp.concatenate([qkv[rows, h * HD : (h + 1) * HD] for h in range(QHEADS)], axis=0)
        g2 = jnp.concatenate([g_ref[rows, h * HD : (h + 1) * HD] for h in range(QHEADS)], axis=0)
        keys = qkv[:extent, NQ : NQ + HD]
        values = qkv[:extent, NQ + HD :]
        nt = (((1,), (1,)), ((), ()))
        scores = lax.dot_general(keys, q2, nt, preferred_element_type=f32)
        dots = lax.dot_general(values, g2, nt, preferred_element_type=f32)
        query = qrow[i : i + 1, :]
        behind = query - kcol[:extent, :]
        allowed = (behind >= 0) & (behind < WINDOW)
        allowed = jnp.concatenate([allowed] * QHEADS, axis=1)
        query = jnp.concatenate([query] * QHEADS, axis=1)
        scores = jnp.where(allowed, scores, neg_fill)
        top = jnp.max(scores, axis=0, keepdims=True)
        expo = jnp.exp((scores - top) * score_scale)
        total = jnp.sum(expo, axis=0, keepdims=True)
        weighted = jnp.sum(expo * dots, axis=0, keepdims=True)
        inverse = jnp.where(query >= 0, 1.0 / total, 0.0)
        delta = weighted * inverse
        probs = expo * inverse
        mixed = (probs * (dots - delta)).astype(bf16)
        probs = probs.astype(bf16)
        dkey = jnp.dot(mixed, q2, preferred_element_type=f32)
        dval = jnp.dot(probs, g2, preferred_element_type=f32)
        before = i * block
        if before:
            dk[:before, :] += dkey[:before]
            dv[:before, :] += dval[:before]
        dk[before:extent, :] = dkey[before:]
        dv[before:extent, :] = dval[before:]
        dq = score_scale * jnp.dot(kt[:, :extent], mixed, preferred_element_type=f32)
        for h in range(QHEADS):
            dq_h = dq[:, h * block : (h + 1) * block].T
            out[rows, h * HD : (h + 1) * HD] = rotate(dq_h, cos_ref[rows, :], -sin_ref[rows, :]).astype(bf16)
    out[:, NQ : NQ + HD] = rotate(score_scale * dk[...], cos_ref[...], -sin_ref[...]).astype(bf16)
    out[:, NQ + HD :] = dv[...].astype(bf16)


def weight_kernel(z, cols, xt, g_ref, *refs):
    pieces, whole = (refs[:-1], refs[-1])
    if whole.shape[0] > z.win:
        whole[z.win :, :] = jnp.zeros_like(whole[z.win :, :])
    inset = z.inset(lax.axis_index("ctx"))
    mine = lax.axis_index("dp") & (QUAD - 1)
    whole[: z.win, :] = jnp.dot(xt[...], g_ref[:, cols], preferred_element_type=f32)
    for k in range(QUAD):
        at = pl.multiple_of(inset + (mine ^ k) * z.chunk, 16)
        pieces[k][...] = whole[pl.ds(at, z.chunk), :].astype(bf16)


def sum_kernel(*refs):
    refs[-1][...] = functools.reduce(lambda a, b: a + b, [r[...].astype(f32) for r in refs[:-1]]).astype(bf16)


def gated(kernel, inputs):
    def with_gates(*refs):
        kernel(*refs[:inputs], *refs[inputs + 1 :])

    return with_gates


def total_of(pieces, gate=None):
    out = shape(pieces[0].shape, bf16)
    if gate is None:
        return call(sum_kernel, out, flops=SUM_COST)(*pieces)
    specs = [pl.BlockSpec(memory_space=pltpu.VMEM)] * len(pieces) + [pl.BlockSpec(memory_space=pl.ANY)]
    return call(gated(sum_kernel, len(pieces)), out, flops=SUM_COST, in_specs=specs)(*pieces, gate)


def inputs_kernel(z, g_ref, w_ref, _, near, far, rows):
    half = z.slots // 2
    for k in range(z.n):
        rows[k * z.cap : (k + 1) * z.cap, :] = g_ref[z.block(k), :]
    nt = (((1,), (1,)), ((), ()))
    far[...] = lax.dot_general(rows[half:, :], w_ref[...], nt, preferred_element_type=f32).astype(bf16)
    near[...] = lax.dot_general(rows[:half, :], w_ref[...], nt, preferred_element_type=f32).astype(bf16)


def place_weight_kernel(z, split, *refs):
    pieces, (out, whole, sems) = (refs[:QUAD], refs[-3:])
    mine = lax.axis_index("dp") & (QUAD - 1)
    wide = z.qkv // SPLITS
    cols = pl.ds(split * wide, wide)
    if QUAD * z.chunk == z.rows:
        copies = []
        for k in range(QUAD):
            rows = pl.ds(pl.multiple_of((mine ^ k) * z.chunk, 16), z.chunk)
            whole[rows, :] = pieces[k][...].astype(f32)
            copies.append(pltpu.make_async_copy(whole.at[rows, :], out.at[rows, cols], sems.at[k]))
            copies[-1].start()
    else:
        for k in range(QUAD):
            at = pl.multiple_of((mine ^ k) * z.chunk, 16)
            whole[pl.ds(at, z.chunk), :] = pieces[k][...].astype(f32)
        copies = [pltpu.make_async_copy(whole.at[: z.rows, :], out.at[:, cols], sems.at[0])]
        copies[0].start()
    for copy in copies:
        copy.wait()


def place_weights(z, split, pieces, before):
    wide = z.qkv // SPLITS
    more = {"input_output_aliases": {QUAD: 0}} if split else {}
    return call(
        functools.partial(place_weight_kernel, z, split),
        shape((z.rows, z.qkv), f32),
        [pltpu.VMEM((QUAD * z.chunk, wide), f32), pltpu.SemaphoreType.DMA((QUAD,))],
        flops=SUM_COST,
        in_specs=[pl.BlockSpec(memory_space=pltpu.VMEM)] * QUAD + [pl.BlockSpec(memory_space=pl.ANY)],
        out_specs=pl.BlockSpec(memory_space=pl.ANY),
        **more,
    )(*pieces, before)


def place_inputs_kernel(z, items, *refs):
    arrays, out = (refs[:-1], refs[-1])
    me = lax.axis_index("ctx")
    out[...] = jnp.zeros_like(out)
    for which, at, source in items:
        cols = pl.ds(z.first(me ^ source), z.win)
        out[:, cols] = out[:, cols] + arrays[which][at : at + z.cap, :]


def gather_packs(pack, n, first):
    order, mask = ([0], n // 2)
    came = first
    while mask:
        pack = jnp.concatenate([pack, came], axis=0)
        order = order + [k ^ mask for k in order]
        mask //= 2
        if mask:
            came = swap(pack, "ctx", mask)
    return pack, order


def exchange_inputs(z, near, far):
    arrays = [near]
    held = {(k, 0): (0, k * z.cap) for k in range(z.n // 2)}
    mask, sent = (z.n // 2, [(k, 0) for k in range(z.n // 2, z.n)])
    parcel = far
    while True:
        arrays.append(swap(parcel, "ctx", mask))
        for i, (k, j) in enumerate(sent):
            held[k ^ mask, j ^ mask] = (len(arrays) - 1, i * z.cap)
        mask //= 2
        if not mask:
            break
        sent = sorted(item for item in held if item[0] & mask)
        spots = [held.pop(item) for item in sent]
        parcel = jnp.concatenate([arrays[which][at : at + z.cap] for which, at in spots], axis=0)
    return arrays, [(which, at, j) for (k, j), (which, at) in sorted(held.items())]


def body(hidden_in, w_qkv, d_attn, range_len, doc_ids):
    tokens = hidden_in[0]
    z = Sizes(tokens, w_qkv)
    n, cap, slots, qkv, win = (z.n, z.cap, z.slots, z.qkv, z.win)
    any_spec = pl.BlockSpec(memory_space=pl.ANY)
    vmem_spec = pl.BlockSpec(memory_space=pltpu.VMEM)

    extra = jnp.concatenate([doc_ids[0], jnp.broadcast_to(range_len[0, 0], (cap,))]).astype(bf16)
    pack = jnp.concatenate([d_attn[0], jnp.broadcast_to(extra[None], (EXTRA, NQ))], axis=0)
    cut = call(
        functools.partial(windows_kernel, z),
        [shape((cap, win), bf16)] * (n - 1),
        [pltpu.SemaphoreType.DMA((n - 1,))],
        moved=6 * cap * win,
        in_specs=[any_spec],
        out_specs=[any_spec] * (n - 1),
    )(tokens)
    xs = [swap(cut[k - 1], "ctx", k) for k in range(1, n)]
    pack_came = swap(pack, "ctx", n // 2)
    w_pad = call(functools.partial(pad_kernel, z), shape((win, qkv), bf16), moved=4 * win * qkv)(w_qkv)
    keep0, send0 = call(
        functools.partial(near_kernel, z),
        [shape((cap, qkv), f32), shape((cap, qkv), bf16)],
        flops=4 * cap * win * qkv,
        moved=4 * win * (cap + qkv),
    )(tokens, xs[0], w_pad)
    sum0 = keep0 + swap(send0, "ctx", 1).astype(f32)
    far_rows = (n // 2 - 1) * cap
    half0 = sum0.astype(bf16)
    cross0 = swap(half0, "ctx", 2)
    packs, order = gather_packs(pack, n, after(pack_came, sum0))
    grads, qrow, kcol, poscol = call(
        functools.partial(spread_kernel, z, order),
        [
            shape((slots, NQ), bf16),
            shape((n, cap), jnp.int32),
            shape((slots, LANES), jnp.int32),
            shape((slots, HD), f32),
        ],
        moved=8 * slots * NQ,
    )(packs)
    lane = jnp.arange(HD, dtype=jnp.int32)
    freqs = 10000.0 ** (-((lane % (HD // 2)).astype(f32) * 2.0) / HD)
    angles = poscol * freqs[None, :]
    cosine = jnp.cos(angles)
    sine = jnp.where(lane < HD // 2, -1.0, 1.0)[None, :] * jnp.sin(angles)

    send1 = call(
        functools.partial(odd_kernel, z),
        shape((far_rows, qkv), bf16),
        flops=2 * far_rows * win * qkv,
        in_specs=[vmem_spec] * (n // 2) + [any_spec],
    )(*xs[2::2], w_pad, half0)
    sum1, half1 = call(
        functools.partial(even_kernel, z),
        [shape((far_rows, qkv), f32), shape((far_rows, qkv), bf16)],
        flops=2 * far_rows * win * qkv,
    )(*xs[1::2], w_pad, swap(send1, "ctx", 1))
    cross1 = swap(half1, "ctx", 2)
    kept = [sum0] + [sum1[i * cap : (i + 1) * cap] for i in range(n // 2 - 1)]
    came = [cross0] + [cross1[i * cap : (i + 1) * cap] for i in range(n // 2 - 1)]
    came = [came[i ^ 1] for i in range(n // 2)]
    mask = 4
    while mask < n:
        both = jnp.concatenate([a + b.astype(f32) for a, b in zip(kept, came)], axis=0)
        crossed = swap(both.astype(bf16), "ctx", mask)
        kept = [both[i * cap : (i + 1) * cap] for i in range(n // 2)]
        came = [crossed[i * cap : (i + 1) * cap] for i in range(n // 2)]
        came = [came[i ^ (mask // 2)] for i in range(n // 2)]
        mask *= 2
    xt = call(functools.partial(transpose_kernel, z), shape((win, slots), bf16), moved=4 * win * slots)(tokens, *xs)
    mine = call(functools.partial(rotary_kernel, z), shape((slots // 2, qkv), bf16), moved=4 * slots * qkv)(
        *kept, *came, cosine, sine
    )
    theirs = swap(mine, "ctx", 1)
    d_proj = call(
        functools.partial(attention_kernel, z),
        shape((slots, qkv), bf16),
        [pltpu.VMEM((slots, qkv), bf16), pltpu.VMEM((slots, HD), f32), pltpu.VMEM((slots, HD), f32)],
        flops=20 * slots * slots * HD,
        moved=8 * slots * qkv,
    )(mine, theirs, grads, qrow, kcol, cosine, sine)

    wide = qkv // SPLITS
    deep = max(win, win - z.rows + QUAD * z.chunk)
    sums = []
    near = far = None
    for s in range(SPLITS):
        own = call(
            functools.partial(weight_kernel, z, slice(s * wide, (s + 1) * wide)),
            [shape((z.chunk, wide), bf16)] * QUAD,
            [pltpu.VMEM((deep, wide), f32)],
            flops=2 * win * slots * wide,
            moved=4 * win * slots,
        )(xt, d_proj)
        pieces = [own[0]] + [swap(own[k], "dp", k) for k in range(1, QUAD)]
        sums.append(total_of(pieces, far))
        if s == 0:
            near, far = call(
                functools.partial(inputs_kernel, z),
                [shape((slots // 2, win), bf16)] * 2,
                [pltpu.VMEM((slots, qkv), bf16)],
                flops=2 * win * slots * qkv,
                moved=4 * win * slots,
                in_specs=[vmem_spec, vmem_spec, any_spec],
            )(d_proj, w_pad, sums[0])
    arrays, items = exchange_inputs(z, near, far)
    totals = []
    for s in range(SPLITS):
        part, mask = (sums[s], QUAD)
        while mask < lax.axis_size("dp"):
            part = total_of([part, swap(part, "dp", mask)], arrays[1] if s else None)
            mask *= 2
        totals.append(part)
    d_x = call(
        functools.partial(place_inputs_kernel, z, items), shape((cap, z.width), bf16), flops=SUM_COST
    )(*arrays)
    d_w = d_x
    for s in range(SPLITS):
        d_w = place_weights(z, s, [totals[s]] + [swap(totals[s], "dp", k) for k in range(1, QUAD)], d_w)
    return (d_x[None], d_w)


def solution(mesh):
    return jax.shard_map(
        body,
        mesh=mesh,
        in_specs=(
            P("dp", "ctx", None),
            P("ctx", None),
            P("dp", "ctx", None),
            P("dp", "ctx"),
            P("dp", "ctx"),
        ),
        out_specs=(P("dp", "ctx", None), P("ctx", None)),
        check_vma=False,
    )
```

```python
import functools

import jax
import jax.numpy as jnp
from jax import lax
from jax.experimental import pallas as pl
from jax.experimental.pallas import tpu as pltpu
from jax.sharding import PartitionSpec as P

HD = 128
WINDOW = 1024
QHEADS = 2
NQ = QHEADS * HD
LANES = 128
QUAD = 4
SPLITS = 2
SEND_ORDER = (2, 1, 3)
EXTRA = 16
AWAITED = 8
DOC_STEP = 1 << 20
VMEM_BYTES = 48 * 1024 * 1024

score_scale = 168.0 ** (-0.5)
neg_fill = -1e30
f32 = jnp.float32
bf16 = jnp.bfloat16


def swap(value, axis, mask):
    count = lax.axis_size(axis)
    return lax.ppermute(value, axis, [(i, i ^ mask) for i in range(count)])


def rotate(values, cosine, sine):
    return values * cosine + pltpu.roll(values, HD // 2, 1) * sine


def call(kernel, out_shape, operands, cost=0, scratch=(), after=(), **more):
    gates = [gate for gate in after if gate is not None]
    count = len(operands)

    def with_gates(*refs):
        kernel(*refs[:count], *refs[count + len(gates) :])

    specs = more.pop("in_specs", [pl.BlockSpec(memory_space=pltpu.VMEM)] * count)
    return pl.pallas_call(
        with_gates,
        out_shape=out_shape,
        in_specs=[*specs, *[pl.BlockSpec(memory_space=pl.ANY)] * len(gates)],
        scratch_shapes=list(scratch),
        compiler_params=pltpu.CompilerParams(vmem_limit_bytes=VMEM_BYTES),
        cost_estimate=pl.CostEstimate(flops=int(cost * 1e9), bytes_accessed=0, transcendentals=0),
        **more,
    )(*operands, *gates)


def shape(dims, dtype):
    return jax.ShapeDtypeStruct(dims, dtype)


class Sizes:
    def __init__(self, tokens, w_qkv):
        self.n = lax.axis_size("ctx")
        self.cap, self.width = tokens.shape
        self.rows, self.qkv = w_qkv.shape
        self.slots = self.n * self.cap
        self.tiles = self.width // LANES
        self.need = self.most_tiles(self.n, self.rows)
        self.need_pair = self.most_tiles(self.n // 2, 2 * self.rows)
        self.win = self.need * LANES
        self.win_pair = self.need_pair * LANES
        self.exact_pairs = 2 * self.rows == self.win_pair
        self.chunk = -(-self.rows // (QUAD * 16)) * 16

    @staticmethod
    def most_tiles(count, rows):
        return max(-(-(c + 1) * rows // LANES) - c * rows // LANES for c in range(count))

    def pair_tile(self, c):
        return jnp.minimum((c // 2) * 2 * self.rows // LANES, self.tiles - self.need_pair)

    def first_pair(self, c):
        return pl.multiple_of(self.pair_tile(c) * LANES, LANES)

    def in_pair(self, c):
        tile = jnp.minimum(c * self.rows // LANES - self.pair_tile(c), self.need_pair - self.need)
        return pl.multiple_of(tile * LANES, LANES)

    def first(self, c):
        return pl.multiple_of(self.first_pair(c) + self.in_pair(c), LANES)

    def inset(self, c):
        return pl.multiple_of(c * self.rows - self.first(c), 16)

    def inset_pair(self, c):
        return pl.multiple_of(c * self.rows - self.first_pair(c), 16)

    def block(self, k):
        return pl.ds(pl.multiple_of((lax.axis_index("ctx") ^ k) * self.cap, self.cap), self.cap)


def windows_kernel(z, x_ref, *refs):
    outs, sems = (refs[: z.n - 1], refs[z.n - 1])
    me = lax.axis_index("ctx")
    copies = [
        pltpu.make_async_copy(x_ref.at[:, pl.ds(z.first(me ^ k), z.win)], outs[k - 1], sems.at[k - 1])
        for k in range(1, z.n)
    ]
    for copy in copies:
        copy.start()
    for copy in copies:
        copy.wait()


def pad_kernel(z, w_ref, pad):
    pad[...] = jnp.zeros_like(pad)
    pad[pl.ds(z.inset(lax.axis_index("ctx")), z.rows), :] = w_ref[...]


def pair_kernel(z, own, other, out):
    me = lax.axis_index("ctx")
    if not z.exact_pairs:
        out[...] = jnp.zeros_like(out)
    out[pl.ds(z.inset_pair(me), z.rows), :] = own[...]
    out[pl.ds(z.inset_pair(me ^ 1), z.rows), :] = other[...]


def spread_kernel(z, order, packs, grads, qrow, kcol, poscol):
    me = lax.axis_index("ctx")
    rows = lax.broadcasted_iota(jnp.int32, (z.n, z.cap), 0)
    docs = jnp.zeros((z.n, z.cap), f32)
    lens = jnp.zeros((z.n, z.cap), f32)
    tall = z.cap + EXTRA
    for place, k in enumerate(order):
        at = place * tall
        grads[z.block(k), :] = packs[at : at + z.cap, :]
        extra = packs[at + z.cap : at + tall, :].astype(f32)[:1]
        docs = jnp.where(rows == (me ^ k), extra[:, : z.cap], docs)
        lens = jnp.where(rows == (me ^ k), extra[:, z.cap : 2 * z.cap], lens)
    docs = docs.astype(jnp.int32)
    lens = lens.astype(jnp.int32)
    offset = lax.broadcasted_iota(jnp.int32, (z.n, z.cap), 1)
    start = jnp.zeros((1, z.cap), jnp.int32)
    for c in range(z.n):
        pos = start + offset[c : c + 1]
        live = offset[c : c + 1] < lens[c : c + 1]
        mark = docs[c : c + 1] * DOC_STEP + pos
        qrow[c : c + 1, :] = jnp.where(live, mark, -DOC_STEP)
        at = slice(c * z.cap, (c + 1) * z.cap)
        key = jnp.where(live, mark, 4 * DOC_STEP).astype(f32)
        kcol[at, :] = jnp.broadcast_to(key, (LANES, z.cap)).T.astype(jnp.int32)
        poscol[at, :] = jnp.broadcast_to(pos.astype(f32), (LANES, z.cap)).T
        start = start + lens[c : c + 1]


def near_kernel(z, x_ref, x1_ref, w_ref, keep, send):
    keep[...] = jnp.dot(x_ref[:, pl.ds(z.first(lax.axis_index("ctx")), z.win)], w_ref[...], preferred_element_type=f32)
    send[...] = jnp.dot(x1_ref[...], w_ref[...], preferred_element_type=f32).astype(bf16)


def odd_kernel(z, *refs):
    xs, (w_ref, send) = (refs[:-2], refs[-2:])
    for i, x_ref in enumerate(xs):
        at = slice(i * z.cap, (i + 1) * z.cap)
        send[at, :] = jnp.dot(x_ref[...], w_ref[...], preferred_element_type=f32).astype(bf16)


def even_kernel(z, *refs):
    xs, (w_ref, came, total, send) = (refs[:-4], refs[-4:])
    for i, x_ref in enumerate(xs):
        at = slice(i * z.cap, (i + 1) * z.cap)
        both = jnp.dot(x_ref[...], w_ref[...], preferred_element_type=f32) + came[at, :].astype(f32)
        total[at, :] = both
        send[at, :] = both.astype(bf16)


def transpose_kernel(z, x_ref, *refs):
    xs, out = (refs[: z.n - 1], refs[z.n - 1])
    out[:, z.block(0)] = x_ref[:, pl.ds(z.first(lax.axis_index("ctx")), z.win)].T
    for k in range(1, z.n):
        out[:, z.block(k)] = xs[k - 1][...].T


def rotary_kernel(z, *refs):
    count = z.n // 2
    kept, came, (cos_ref, sin_ref, out) = (refs[:count], refs[count : 2 * count], refs[2 * count :])
    for i in range(count):
        proj = kept[i][...].astype(f32) + came[i][...].astype(f32)
        rows = z.block(2 * i)
        at = slice(i * z.cap, (i + 1) * z.cap)
        cosine, sine = (cos_ref[rows, :], sin_ref[rows, :])
        for h in range(QHEADS + 1):
            cols = slice(h * HD, (h + 1) * HD)
            out[at, cols] = rotate(proj[:, cols], cosine, sine).astype(bf16)
        out[at, NQ + HD :] = proj[:, NQ + HD :].astype(bf16)


def attention_kernel(z, own, other, g_ref, qrow, kcol, cos_ref, sin_ref, out, qkv, dk, dv):
    block = z.cap
    for k in range(z.n):
        source = other if k & 1 else own
        qkv[z.block(k), :] = source[k // 2 * block : (k // 2 + 1) * block, :]
    kt = qkv[:, NQ : NQ + HD].astype(f32).T.astype(bf16)
    for i in range(z.n):
        rows = slice(i * block, (i + 1) * block)
        extent = (i + 1) * block
        q2 = jnp.concatenate([qkv[rows, h * HD : (h + 1) * HD] for h in range(QHEADS)], axis=0)
        g2 = jnp.concatenate([g_ref[rows, h * HD : (h + 1) * HD] for h in range(QHEADS)], axis=0)
        keys = qkv[:extent, NQ : NQ + HD]
        values = qkv[:extent, NQ + HD :]
        nt = (((1,), (1,)), ((), ()))
        scores = lax.dot_general(keys, q2, nt, preferred_element_type=f32)
        dots = lax.dot_general(values, g2, nt, preferred_element_type=f32)
        query = qrow[i : i + 1, :]
        behind = query - kcol[:extent, :]
        allowed = (behind >= 0) & (behind < WINDOW)
        allowed = jnp.concatenate([allowed] * QHEADS, axis=1)
        query = jnp.concatenate([query] * QHEADS, axis=1)
        scores = jnp.where(allowed, scores, neg_fill)
        top = jnp.max(scores, axis=0, keepdims=True)
        expo = jnp.exp((scores - top) * score_scale)
        total = jnp.sum(expo, axis=0, keepdims=True)
        weighted = jnp.sum(expo * dots, axis=0, keepdims=True)
        inverse = jnp.where(query >= 0, 1.0 / total, 0.0)
        delta = weighted * inverse
        probs = expo * inverse
        mixed = (probs * (dots - delta)).astype(bf16)
        probs = probs.astype(bf16)
        dkey = jnp.dot(mixed, q2, preferred_element_type=f32)
        dval = jnp.dot(probs, g2, preferred_element_type=f32)
        before = i * block
        if before:
            dk[:before, :] += dkey[:before]
            dv[:before, :] += dval[:before]
        dk[before:extent, :] = dkey[before:]
        dv[before:extent, :] = dval[before:]
        dq = score_scale * jnp.dot(kt[:, :extent], mixed, preferred_element_type=f32)
        for h in range(QHEADS):
            dq_h = dq[:, h * block : (h + 1) * block].T
            out[rows, h * HD : (h + 1) * HD] = rotate(dq_h, cos_ref[rows, :], -sin_ref[rows, :]).astype(bf16)
    out[:, NQ : NQ + HD] = rotate(score_scale * dk[...], cos_ref[...], -sin_ref[...]).astype(bf16)
    out[:, NQ + HD :] = dv[...].astype(bf16)


def weight_kernel(z, cols, xt, g_ref, *refs):
    pieces, whole = (refs[:-1], refs[-1])
    if whole.shape[0] > z.win:
        whole[z.win :, :] = jnp.zeros_like(whole[z.win :, :])
    inset = z.inset(lax.axis_index("ctx"))
    mine = lax.axis_index("dp") & (QUAD - 1)
    whole[: z.win, :] = jnp.dot(xt[...], g_ref[:, cols], preferred_element_type=f32)
    for k in range(QUAD):
        at = pl.multiple_of(inset + (mine ^ k) * z.chunk, 16)
        pieces[k][...] = whole[pl.ds(at, z.chunk), :].astype(bf16)


def sum_kernel(*refs):
    refs[-1][...] = functools.reduce(lambda a, b: a + b, [r[...].astype(f32) for r in refs[:-1]]).astype(bf16)


def inputs_kernel(z, g_ref, w_ref, near, far, rows):
    half = z.slots // 4
    for i in range(z.n // 2):
        rows[i * z.cap : (i + 1) * z.cap, :] = g_ref[z.block(2 * i), :]
    nt = (((1,), (1,)), ((), ()))
    far[...] = lax.dot_general(rows[half:, :], w_ref[...], nt, preferred_element_type=f32).astype(bf16)
    near[...] = lax.dot_general(rows[:half, :], w_ref[...], nt, preferred_element_type=f32).astype(bf16)


def place_weight_kernel(z, cols, *refs):
    pieces, (out, whole, sems) = (refs[:QUAD], refs[-3:])
    mine = lax.axis_index("dp") & (QUAD - 1)
    copies = []
    for k in range(QUAD):
        at = slice(k * z.chunk, (k + 1) * z.chunk)
        rows = pl.ds(pl.multiple_of((mine ^ k) * z.chunk, 16), z.chunk)
        whole[at, :] = pieces[k][...].astype(f32)
        copies.append(pltpu.make_async_copy(whole.at[at, :], out.at[rows, cols], sems.at[k]))
        copies[-1].start()
    for copy in copies:
        copy.wait()


def place_weights(z, cols, pieces, before, cost, after):
    more = {}
    specs = [pl.BlockSpec(memory_space=pltpu.VMEM)] * QUAD
    if before is not None:
        specs.append(pl.BlockSpec(memory_space=pl.ANY))
        more["input_output_aliases"] = {QUAD: 0}
        pieces = [*pieces, before]
    return call(
        functools.partial(place_weight_kernel, z, cols),
        shape((z.rows, z.qkv), f32),
        pieces,
        cost=cost,
        scratch=[pltpu.VMEM((QUAD * z.chunk, cols.stop - cols.start), f32), pltpu.SemaphoreType.DMA((QUAD,))],
        after=after,
        in_specs=specs,
        out_specs=pl.BlockSpec(memory_space=pl.ANY),
        **more,
    )


def place_all_kernel(z, bounds, *refs):
    pieces, (out, whole) = (refs[:-2], refs[-2:])
    mine = lax.axis_index("dp") & (QUAD - 1)
    for i, piece in enumerate(pieces):
        split, k = divmod(i, QUAD)
        at = pl.multiple_of((mine ^ k) * z.chunk, 16)
        whole[pl.ds(at, z.chunk), bounds[split]] = piece[...].astype(f32)
    out[...] = whole[: z.rows, :]


def place_inputs_kernel(z, items, *refs):
    arrays, out = (refs[:-1], refs[-1])
    me = lax.axis_index("ctx")
    if not z.exact_pairs:
        out[...] = jnp.zeros_like(out)
    for which, at, source in items:
        cols = pl.ds(z.first_pair(me ^ source), z.win_pair)
        window = arrays[which][at : at + z.cap, :]
        out[:, cols] = window if z.exact_pairs else out[:, cols] + window


def gather_packs(pack, came, n):
    order, mask = ([0], n // 2)
    while mask:
        pack = jnp.concatenate([pack, came], axis=0)
        order = order + [k ^ mask for k in order]
        mask //= 2
        if mask:
            came = swap(pack, "ctx", mask)
    return pack, order


def exchange_inputs(z, near, far):
    step = 2
    arrays = [near]
    held = {(k, 0): (0, i * z.cap) for i, k in enumerate(range(0, z.n // 2, step))}
    mask, sent = (z.n // 2, [(k, 0) for k in range(z.n // 2, z.n, step)])
    parcel = far
    while True:
        arrays.append(swap(parcel, "ctx", mask))
        for i, (k, j) in enumerate(sent):
            held[k ^ mask, j ^ mask] = (len(arrays) - 1, i * z.cap)
        mask //= 2
        if mask < step:
            break
        sent = sorted(item for item in held if item[0] & mask)
        spots = [held.pop(item) for item in sent]
        parcel = jnp.concatenate([arrays[which][at : at + z.cap] for which, at in spots], axis=0)
    return arrays, [(which, at, j) for (k, j), (which, at) in sorted(held.items())]


def body(hidden_in, w_qkv, d_attn, range_len, doc_ids):
    tokens = hidden_in[0]
    z = Sizes(tokens, w_qkv)
    n, cap, slots, qkv, win = (z.n, z.cap, z.slots, z.qkv, z.win)
    any_spec = pl.BlockSpec(memory_space=pl.ANY)

    extra = jnp.concatenate([doc_ids[0], jnp.broadcast_to(range_len[0, 0], (cap,))]).astype(bf16)
    pack = jnp.concatenate([d_attn[0], jnp.broadcast_to(extra[None], (EXTRA, NQ))], axis=0)
    cut = call(
        functools.partial(windows_kernel, z),
        [shape((cap, win), bf16)] * (n - 1),
        [tokens],
        cost=0.34,
        scratch=[pltpu.SemaphoreType.DMA((n - 1,))],
        in_specs=[any_spec],
        out_specs=[any_spec] * (n - 1),
    )
    xs = [swap(cut[k - 1], "ctx", k) for k in range(1, n)]
    w_pad = call(functools.partial(pad_kernel, z), shape((win, qkv), bf16), [w_qkv], cost=0.9)
    keep0, send0 = call(
        functools.partial(near_kernel, z),
        [shape((cap, qkv), f32), shape((cap, qkv), bf16)],
        [tokens, xs[0], w_pad],
        cost=1.1,
    )
    sum0 = keep0 + swap(send0, "ctx", 1).astype(f32)
    half0 = sum0.astype(bf16)
    cross0 = swap(half0, "ctx", 2)
    pack_came = swap(pack, "ctx", n // 2)
    pack_came = lax.optimization_barrier((pack_came, sum0))[0]
    packs, order = gather_packs(pack, pack_came, n)
    grads, qrow, kcol, poscol = call(
        functools.partial(spread_kernel, z, order),
        [
            shape((slots, NQ), bf16),
            shape((n, cap), jnp.int32),
            shape((slots, LANES), jnp.int32),
            shape((slots, HD), f32),
        ],
        [packs],
        cost=0.33,
    )
    lane = jnp.arange(HD, dtype=jnp.int32)
    freqs = 10000.0 ** (-((lane % (HD // 2)).astype(f32) * 2.0) / HD)
    angles = poscol * freqs[None, :]
    cosine = jnp.cos(angles)
    sine = jnp.where(lane < HD // 2, -1.0, 1.0)[None, :] * jnp.sin(angles)

    far_rows = (n // 2 - 1) * cap
    send1 = call(
        functools.partial(odd_kernel, z),
        shape((far_rows, qkv), bf16),
        [*xs[2::2], w_pad],
        cost=0.21,
        after=[half0],
    )
    sum1, half1 = call(
        functools.partial(even_kernel, z),
        [shape((far_rows, qkv), f32), shape((far_rows, qkv), bf16)],
        [*xs[1::2], w_pad, swap(send1, "ctx", 1)],
        cost=0.21,
    )
    cross1 = swap(half1, "ctx", 2)
    kept = [sum0] + [sum1[i * cap : (i + 1) * cap] for i in range(n // 2 - 1)]
    came = [cross0] + [cross1[i * cap : (i + 1) * cap] for i in range(n // 2 - 1)]
    came = [came[i ^ 1] for i in range(n // 2)]
    mask = 4
    while mask < n:
        both = jnp.concatenate([a + b.astype(f32) for a, b in zip(kept, came)], axis=0)
        crossed = swap(both.astype(bf16), "ctx", mask)
        kept = [both[i * cap : (i + 1) * cap] for i in range(n // 2)]
        came = [crossed[i * cap : (i + 1) * cap] for i in range(n // 2)]
        came = [came[i ^ (mask // 2)] for i in range(n // 2)]
        mask *= 2
    xt = call(functools.partial(transpose_kernel, z), shape((win, slots), bf16), [tokens, *xs], cost=0.9)
    w_pair = call(
        functools.partial(pair_kernel, z),
        shape((z.win_pair, qkv), bf16),
        [w_qkv, swap(w_qkv, "ctx", 1)],
        cost=0.9,
        after=[half0],
    )
    mine = call(
        functools.partial(rotary_kernel, z),
        shape((slots // 2, qkv), bf16),
        [*kept, *came, cosine, sine],
        cost=0.33,
    )
    theirs = swap(mine, "ctx", 1)
    d_proj = call(
        functools.partial(attention_kernel, z),
        shape((slots, qkv), bf16),
        [mine, theirs, grads, qrow, kcol, cosine, sine],
        cost=0.77,
        scratch=[pltpu.VMEM((slots, qkv), bf16), pltpu.VMEM((slots, HD), f32), pltpu.VMEM((slots, HD), f32)],
    )

    deep = max(win, win - z.rows + QUAD * z.chunk)
    wide = qkv // SPLITS
    bounds = [slice(s * wide, (s + 1) * wide) for s in range(SPLITS)]

    def weight_pieces(split):
        own = call(
            functools.partial(weight_kernel, z, bounds[split]),
            [shape((z.chunk, wide), bf16)] * QUAD,
            [xt, d_proj],
            cost=0.9,
            scratch=[pltpu.VMEM((deep, wide), f32)],
        )
        came = {k: swap(own[k], "dp", k) for k in SEND_ORDER}
        return [own[0]] + [came[k] for k in range(1, QUAD)]

    def add_up(pieces, after=()):
        return call(sum_kernel, shape((z.chunk, wide), bf16), pieces, cost=AWAITED, after=after)

    first = weight_pieces(0)
    sums = [add_up(first)]
    second = weight_pieces(1)
    near, far = call(
        functools.partial(inputs_kernel, z),
        [shape((slots // 4, z.win_pair), bf16)] * 2,
        [d_proj, w_pair],
        cost=0.9,
        scratch=[pltpu.VMEM((slots // 2, qkv), bf16)],
        after=[first[2]],
    )
    sums.append(add_up(second, after=[far]))
    arrays, items = exchange_inputs(z, near, far)
    totals = []
    for s in range(SPLITS):
        part, mask = (sums[s], QUAD)
        while mask < lax.axis_size("dp"):
            part = add_up([part, swap(part, "dp", mask)], after=[arrays[1]] if s else [])
            mask *= 2
        totals.append(part)
    d_x = call(
        functools.partial(place_inputs_kernel, z, items),
        shape((cap, z.width), bf16),
        arrays,
        cost=AWAITED,
        after=[totals[0]],
    )
    ready = []
    for total in totals:
        came = {k: swap(total, "dp", k) for k in SEND_ORDER}
        ready.append([total] + [came[k] for k in range(1, QUAD)])
    if QUAD * z.chunk == z.rows:
        d_w = place_weights(z, bounds[0], ready[0], None, AWAITED, [d_x])
        d_w = place_weights(z, bounds[1], ready[1], d_w, 0, [])
    else:
        d_w = call(
            functools.partial(place_all_kernel, z, bounds),
            shape((z.rows, qkv), f32),
            sum(ready, []),
            scratch=[pltpu.VMEM((QUAD * z.chunk, qkv), f32)],
        )
    return (d_x[None], d_w)


def solution(mesh):
    return jax.shard_map(
        body,
        mesh=mesh,
        in_specs=(
            P("dp", "ctx", None),
            P("ctx", None),
            P("dp", "ctx", None),
            P("dp", "ctx"),
            P("dp", "ctx"),
        ),
        out_specs=(P("dp", "ctx", None), P("ctx", None)),
        check_vma=False,
    )
```
